32 devices in a mesh: groups: 2 (over y), expert: 4 (over z), tensor: 2 (over x), dp: 2 (over core).
Axes of the slice: x: 2, y: 2, z: 4, core: 2. Of those that a mesh axis runs over, the one named last changes fastest.
Arguments:
- attn: bfloat16 [1024, 4096], P(('groups', 'expert', 'dp'), 'tensor'), parts along dimension 0, may hold values from -6 to 6
- o_weight: bfloat16 [4096, 4096], P('tensor', 'dp'), may hold values from -0.09375 to 0.09375
- residual: bfloat16 [1024, 4096], P(('groups', 'expert', 'dp'), 'tensor'), parts along dimension 0, may hold values from -100 to 100
- norm_gain: bfloat16 [4096], replicated, may hold values from 0.099609375 to 1.8984375
- expert_ids: int32 [1024, 8], P(('groups', 'expert', 'dp')), parts along dimension 0, may hold values from 0 to 31, all different within a row; in each aligned block of 64 rows (0 to 63, 64 to 127, ...) at most 24 rows name the same one
- route_weights: float32 [1024, 8], P(('groups', 'expert', 'dp')), parts along dimension 0, may hold values from 0.1 to 1
- w_gate: bfloat16 [32, 4096, 1024], P(('expert', 'dp'), None, 'tensor'), may hold values from -0.09375 to 0.09375
- w_up: bfloat16 [32, 4096, 1024], P(('expert', 'dp'), None, 'tensor'), may hold values from -0.09375 to 0.09375
- w_down: bfloat16 [32, 1024, 4096], P(('expert', 'dp'), 'tensor'), may hold values from -0.25 to 0.25
Outputs:
- moe_out: bfloat16 [1024, 4096], P(('groups', 'expert', 'dp'), 'tensor'), parts along dimension 0
The draws below stay inside these ranges and needn't reach their ends.
There are 2 independent parts, one for each index of `groups`. The reference program is written for one: setup_inputs(seed, part) draws one part's arguments, and reference() takes and returns one part's arrays. A program takes and returns all parts, laid end to end along the dimension named above; an argument that names none is the same for every part. Nothing has to cross between parts.
Inputs may be any that keep to these rules, and one draw needn't show every extreme that they name: `expert_ids`: each row names 8 different experts. Within each aligned block of 64 rows (the rows of one device) no expert is named by more than 24 rows, and in every draw some block has an expert named by exactly 24 rows.
All inputs are finite; a program needn't handle non-finite values.
Results may differ from the reference program's by a relative error of at most 0.024.
Values may be sent and summed in bfloat16 or wider, within the bound.
A program may use at most 128 MiB of HBM per device.

```python
import math
import jax
import jax.numpy as jnp
import numpy as np
from jax import lax

D = 4096
HA = 4096
FF = 1024
EXPERTS = 32
TOPK = 8
ROWS_DEV = 64
SLOT = 24
ROWS = 512
FF_PART = 512
N_TENSOR = 2


def draw_residual(key, part):
    key_base, key_row = jax.random.split(jax.random.fold_in(key, 17), 2)
    column_scale = 0.3 * 10.0 ** (jnp.arange(D, dtype=jnp.float32) / D)
    base = jax.random.normal(key_base, (ROWS, D), jnp.float32)
    row_scale = jnp.exp(jax.random.uniform(key_row, (ROWS, 1), jnp.float32, jnp.log(0.5), jnp.log(5.0)))
    return jnp.clip(base * row_scale * column_scale[None, :], -100.0, 100.0).astype(jnp.bfloat16)


def with_spikes(entries, key, source, target, blocks, factor):
    owner, partner = [(jnp.arange(entries.shape[position]) // (entries.shape[position] // blocks)).reshape([-1 if axis == position else 1 for axis in range(entries.ndim)]) for position in (source, target)]
    chosen = jax.random.permutation(key, blocks)[partner]
    strong = (owner == chosen) | (owner == (partner + blocks // 2) % blocks)
    return jnp.where(strong, factor * entries, entries)


def level_of(stream_key, shape, pieces, smallest, high):
    level = 1.0
    for dim, parts in pieces:
        draws = jax.random.uniform(jax.random.fold_in(jax.random.fold_in(stream_key, 6), dim), (parts,), jnp.float32, smallest / len(pieces), high / len(pieces))
        level = level * jnp.repeat(jnp.exp(draws), shape[dim] // parts).reshape((-1,) + (1,) * (len(shape) - 1 - dim))
    return level


def deal_out(key, own, number, rows, number_of, top, most, lean):
    sequence = jax.random.permutation(key, number_of)
    crowded, ordinary = portions_of(number_of, rows * top, most, lean, True), portions_of(number_of, rows * top, most, lean, False)
    places = jnp.arange(number_of)

    def named(lengths, turn):
        used = int((lengths > 0).sum())
        fixed = max(1, used // 4)
        passed = fixed + (places - fixed + turn * (used - fixed)) % max(1, number_of - fixed)
        return jnp.zeros((number_of,), jnp.int32).at[sequence[jnp.where(places < fixed, places, passed)]].set(jnp.asarray(lengths, jnp.int32))

    lengths = jnp.where(number % 4 == 0, named(crowded, number // 4), named(ordinary, number - number // 4 - 1))
    mixed = jax.random.permutation(jax.random.fold_in(own, 3), number_of)
    giver, sink = mixed[0:number_of // 2 * 2:2], mixed[1:number_of // 2 * 2:2]
    margin = jnp.minimum(lengths[giver] - 1, most - lengths[sink]) // 2
    margin = jnp.where((giver == sequence[0]) | (sink == sequence[0]) | (lengths[sink] == 0), 0, jnp.maximum(margin, 0))
    passed = jax.random.randint(jax.random.fold_in(own, 4), (number_of // 2,), 0, 1 << 20) % (margin + 1)
    lengths = lengths.at[giver].add(-passed).at[sink].add(passed)
    items = jnp.searchsorted(jnp.cumsum(lengths), jnp.arange(rows * top), side="right").astype(jnp.int32)
    table = items.reshape(top, rows).T
    table = table[jax.random.permutation(jax.random.fold_in(own, 1), rows)]
    turn = jax.random.randint(jax.random.fold_in(own, 2), (rows, 1), 0, top)
    return jnp.take_along_axis(table, (jnp.arange(top)[None, :] + turn) % top, axis=1)


def portions_of(count, total, limit, lean, full):
    portions = [(1 << 20) // math.isqrt(standing ** lean) + 1 for standing in range(1, count + 1)]
    largest = limit if full else min(limit, max(-(-total // count), total * portions[0] // sum(portions)))
    least = 1 if total - largest >= count - 1 else 0
    given, rest = [largest] + [least] * (count - 1), total - largest - least * (count - 1)
    while rest > 0:
        movable = [i for i in range(1, count) if given[i] < largest] or [i for i in range(1, count) if given[i] < limit]
        mass, budget = sum([portions[i] for i in movable]), rest
        for i in movable:
            addition = min(limit - given[i], max(1, budget * portions[i] // mass), rest)
            given[i] = given[i] + addition
            rest = rest - addition
    return np.array(given)


def gaussian(stream_key, shape, spread, most, pieces=(), held_as=jnp.bfloat16):
    entries = jax.random.normal(stream_key, shape, jnp.float32) * spread
    if len(pieces) > 0:
        entries = level_of(stream_key, shape, pieces, -0.22, 0.18) * entries
    return jnp.clip(entries, min=-most, max=most).astype(held_as)


def bell_draw_with(rng, extent, width, limit, shards, heavy, held_as=jnp.bfloat16):
    array = width * jax.random.normal(rng, extent, jnp.float32)
    if shards:
        array = array * level_of(rng, extent, shards, -0.22, 0.18)
    return jnp.clip(with_spikes(array, jax.random.fold_in(rng, 3), *heavy), -limit, limit).astype(held_as)


def setup_inputs(seed: int = 0, part: int = 0) -> dict:
    key_list = jax.random.split(jax.random.key(seed), 10)
    part_keys = jax.random.split(jax.random.fold_in(key_list[9], part), 10)
    attn = gaussian(part_keys[0], (ROWS, HA), 1.0, 6.0, ((0, 8), (1, 2)))
    o_weight = gaussian(key_list[1], (HA, D), HA ** -0.5, 0.09375, ((0, 2), (1, 2)))
    residual = draw_residual(jax.random.fold_in(jax.random.fold_in(key_list[9], part), 71), part)
    norm_gain = jnp.clip(1.0 + 0.18 * jax.random.normal(key_list[3], (D,), jnp.float32), 0.099609375, 1.8984375).astype(jnp.bfloat16)
    expert_ids_keys = jax.random.split(jax.random.fold_in(part_keys[4], 1), ROWS // ROWS_DEV)
    expert_ids_turns = jax.random.permutation(jax.random.fold_in(part_keys[4], 3), ROWS // ROWS_DEV)
    expert_ids = jax.vmap(lambda own, number: deal_out(jax.random.fold_in(part_keys[4], 2), own, number, ROWS_DEV, EXPERTS, TOPK, SLOT, 2))(expert_ids_keys, expert_ids_turns).reshape((ROWS, TOPK))
    route_weights = jnp.clip(jnp.exp(math.log(1.0) - 2.3025851 * jax.random.uniform(part_keys[5], (ROWS, TOPK), jnp.float32) ** level_of(part_keys[5], (ROWS, TOPK), ((0, 8),), -0.2, 0.2)), 0.1, 1.0)
    w_gate = gaussian(key_list[6], (EXPERTS, D, FF), D ** -0.5, 0.09375, ((0, 8), (2, 2)))
    w_up = gaussian(key_list[7], (EXPERTS, D, FF), D ** -0.5, 0.09375, ((0, 8), (2, 2)))
    w_down = bell_draw_with(key_list[8], (EXPERTS, FF, D), FF ** -0.5, 0.25, ((0, 8), (1, 2)), (1, 2, 2, 2.0))
    return {"attn": attn, "o_weight": o_weight, "residual": residual, "norm_gain": norm_gain, "expert_ids": expert_ids, "route_weights": route_weights, "w_gate": w_gate, "w_up": w_up, "w_down": w_down}


def run_expert(packed):
    slot_rows, gate_weight, up_weight, down_weight = packed
    gate_acc = jnp.dot(slot_rows, gate_weight, preferred_element_type=jnp.float32)
    up_acc = jnp.dot(slot_rows, up_weight, preferred_element_type=jnp.float32)
    activated = (jax.nn.silu(gate_acc) * up_acc).astype(jnp.bfloat16)
    total = jnp.zeros((slot_rows.shape[0], D), jnp.float32)
    for group in range(N_TENSOR):
        lower_edge = group * FF_PART
        piece_out = jnp.dot(activated[:, lower_edge:lower_edge + FF_PART], down_weight[lower_edge:lower_edge + FF_PART], preferred_element_type=jnp.float32).astype(jnp.bfloat16)
        piece_out = lax.optimization_barrier(piece_out)
        total = total + piece_out.astype(jnp.float32)
    return total.astype(jnp.bfloat16)

def reference(attn, o_weight, residual, norm_gain, expert_ids, route_weights, w_gate, w_up, w_down):
    summed = jnp.dot(attn, o_weight, preferred_element_type=jnp.float32) + residual.astype(jnp.float32)
    rounded = lax.optimization_barrier(summed.astype(jnp.bfloat16))
    hidden_f = rounded.astype(jnp.float32)
    mean_sq = lax.optimization_barrier(jnp.mean(hidden_f * hidden_f, axis=1, keepdims=True))
    normed = (hidden_f * lax.rsqrt(mean_sq + 1e-06) * norm_gain.astype(jnp.float32)).astype(jnp.bfloat16)
    block_count = ROWS // ROWS_DEV
    onehot = (expert_ids[:, :, None] == jnp.arange(EXPERTS, dtype=jnp.int32)).astype(jnp.int32)
    chosen = lax.optimization_barrier(jnp.sum(onehot, axis=1)).reshape(block_count, ROWS_DEV, EXPERTS)
    before = (jnp.cumsum(chosen, axis=1) - chosen).reshape(ROWS, EXPERTS)
    slot_index = lax.optimization_barrier(jnp.sum(onehot * before[:, None, :], axis=2)).astype(jnp.int32)
    block_index = jnp.broadcast_to((jnp.arange(ROWS, dtype=jnp.int32) // ROWS_DEV)[:, None], (ROWS, TOPK)).astype(jnp.int32)
    slots = jnp.zeros((EXPERTS, block_count, SLOT, D), jnp.bfloat16)
    slots = slots.at[expert_ids, block_index, slot_index].set(jnp.broadcast_to(normed[:, None, :], (ROWS, TOPK, D)))
    expert_out = lax.map(run_expert, (slots.reshape(EXPERTS, block_count * SLOT, D), w_gate, w_up, w_down))
    expert_out = expert_out.reshape(EXPERTS, block_count, SLOT, D)
    picked = expert_out[expert_ids, block_index, slot_index].astype(jnp.float32)
    moe_out = lax.optimization_barrier(jnp.sum(route_weights[:, :, None] * picked, axis=1))
    return moe_out.astype(jnp.bfloat16)
```

```python
import functools

import jax
import jax.numpy as jnp
from jax import lax
from jax.experimental import pallas as pl
from jax.experimental.pallas import tpu as pltpu
from jax.sharding import PartitionSpec as P

MESH = pl.DeviceIdType.MESH
epsilon = 1e-06
MIB = 1 << 20


def greet(z, t, d, n_z, n_t, n_d, square):
    barrier = pltpu.get_barrier_semaphore()
    count = 0
    for i in range(n_t):
        for j in range(n_d):
            if (i or j) and (square or not (i and j)):
                pl.semaphore_signal(
                    barrier,
                    inc=1,
                    device_id={"tensor": lax.rem(t + i, n_t), "dp": lax.rem(d + j, n_d)},
                    device_id_type=MESH,
                )
                count += 1
    for i in range(1, n_z):
        pl.semaphore_signal(
            barrier, inc=1, device_id={"expert": lax.rem(z + i, n_z)}, device_id_type=MESH
        )
        count += 1
    pl.semaphore_wait(barrier, count)


def gather_kernel(
    n_z, n_t, n_d, attn, ow_hbm, residual, gain, out,
    pair, ow, part, landed, squares,
    ow_sem, a_send, a_recv, p_send, p_recv, s_send, s_recv,
    z_send, z_recv, x_send, x_recv, c_send, c_recv,
):
    z, t, d = lax.axis_index("expert"), lax.axis_index("tensor"), lax.axis_index("dp")
    rows, depth = attn.shape
    width = residual.shape[1]
    held = ow.shape[1]
    blocks = held // width
    load = pltpu.make_async_copy(ow_hbm, ow, ow_sem)
    load.start()
    greet(z, t, d, n_z, n_t, n_d, True)

    pair[pl.ds(d * rows, rows), :] = attn[...]
    sent = []
    for j in range(1, n_d):
        copy = pltpu.make_async_remote_copy(
            attn, pair.at[pl.ds(d * rows, rows), :], a_send.at[j], a_recv.at[j],
            device_id={"dp": lax.rem(d + j, n_d)}, device_id_type=MESH,
        )
        copy.start()
        sent.append(copy)
    load.wait()
    for copy in sent:
        copy.wait()

    tile = min(512, width)
    for first in range(0, held, tile):
        part[:, pl.ds(first, tile)] = jnp.dot(
            pair[...], ow[:, pl.ds(first, tile)], preferred_element_type=jnp.float32
        ).astype(jnp.bfloat16)

    def piece(i, j):
        owner, core = d * blocks + i, lax.rem(d + j, n_d)
        source = part.at[pl.ds(core * rows, rows), pl.ds(i * width, width)]
        copy = pltpu.make_async_remote_copy(
            source, landed.at[t], p_send.at[i, j], p_recv.at[t],
            device_id={"tensor": owner, "dp": core}, device_id_type=MESH,
        )
        return owner, core, copy

    for i in range(blocks):
        for j in range(n_d):
            owner, core, copy = piece(i, j)
            if j:
                copy.start()
            else:
                @pl.when(owner != t)
                def _():
                    copy.start()

                @pl.when(owner == t)
                def _():
                    landed[t] = part[pl.ds(d * rows, rows), pl.ds(i * width, width)]

    for i in range(n_t):
        arrival = pltpu.make_async_remote_copy(
            landed.at[i], landed.at[i], p_send.at[0, 0], p_recv.at[i],
            device_id={"tensor": i}, device_id_type=MESH,
        )

        @pl.when(jnp.logical_or(i != t, t // blocks != d))
        def _():
            arrival.wait_recv()

    hidden = residual[...].astype(jnp.float32)
    for i in range(n_t):
        hidden = hidden + landed[i].astype(jnp.float32)
    hidden = hidden.astype(jnp.bfloat16).astype(jnp.float32)
    squares[0] = jnp.broadcast_to(
        jnp.sum(hidden * hidden, axis=1, keepdims=True), squares.shape[1:]
    )
    sums = []
    for i in range(1, n_t):
        copy = pltpu.make_async_remote_copy(
            squares.at[0], squares.at[i], s_send.at[i], s_recv.at[i],
            device_id={"tensor": lax.rem(t + i, n_t)}, device_id_type=MESH,
        )
        copy.start()
        sums.append(copy)
    for copy in sums:
        copy.wait()
    total = squares[0]
    for i in range(1, n_t):
        total = total + squares[i]
    inverse = lax.rsqrt(total[:, :1] / (width * n_t) + epsilon)
    columns = pl.ds(pl.multiple_of(t * width, width), width)
    normed = hidden * inverse * gain[:, columns].astype(jnp.float32)

    def block(core, chip, half):
        return out.at[
            pl.ds(pl.multiple_of((core * n_z + chip) * rows, rows), rows),
            pl.ds(pl.multiple_of(half * width, width), width),
        ]

    block(d, z, t)[...] = normed.astype(jnp.bfloat16)

    started = []

    def to_tensor(i, chip):
        copies = []
        for h in range(1, n_t):
            ref = block(d, lax.rem(z - chip + n_z, n_z), t)
            copy = pltpu.make_async_remote_copy(
                ref, ref, x_send.at[h, chip], x_recv.at[h, chip],
                device_id={"tensor": lax.rem(t + h, n_t)}, device_id_type=MESH,
            )
            copy.start()
            copies.append(copy)
        started.extend(copies)

    def to_core(h, chip):
        for j in range(1, n_d):
            ref = block(d, lax.rem(z - chip + n_z, n_z), lax.rem(t - h + n_t, n_t))
            copy = pltpu.make_async_remote_copy(
                ref, ref, c_send.at[j, h, chip], c_recv.at[j, h, chip],
                device_id={"dp": lax.rem(d + j, n_d)}, device_id_type=MESH,
            )
            copy.start()
            started.append(copy)

    to_tensor(t, 0)
    order = sorted(range(1, n_z), key=lambda i: min(i, n_z - i))
    for i in order:
        ref = block(d, z, t)
        copy = pltpu.make_async_remote_copy(
            ref, ref, z_send.at[i], z_recv.at[i],
            device_id={"expert": lax.rem(z + i, n_z)}, device_id_type=MESH,
        )
        copy.start()
        started.append(copy)
    to_core(0, 0)

    def await_block(ref, sem):
        pltpu.make_async_remote_copy(
            ref, ref, z_send.at[0], sem, device_id={"tensor": t}, device_id_type=MESH
        ).wait_recv()

    def from_tensor(chip):
        for h in range(1, n_t):
            await_block(
                block(d, lax.rem(z - chip + n_z, n_z), lax.rem(t - h + n_t, n_t)),
                x_recv.at[h, chip],
            )
            to_core(h, chip)

    for i in order:
        await_block(block(d, lax.rem(z - i + n_z, n_z), t), z_recv.at[i])
        to_tensor(t, i)
        to_core(0, i)
    for i in [0] + order:
        from_tensor(i)
    for i in [0] + order:
        for h in range(n_t):
            for j in range(1, n_d):
                await_block(
                    block(
                        lax.rem(d - j + n_d, n_d),
                        lax.rem(z - i + n_z, n_z),
                        lax.rem(t - h + n_t, n_t),
                    ),
                    c_recv.at[j, h, i],
                )
    for copy in started:
        copy.wait_send()
    for i in range(blocks):
        for j in range(n_d):
            owner, core, copy = piece(i, j)
            if j:
                copy.wait_send()
            else:
                @pl.when(owner != t)
                def _():
                    copy.wait_send()


def experts_kernel(x, gate, up, weight, out):
    j = pl.program_id(0)
    lane = lax.broadcasted_iota(jnp.int32, weight.shape, 1)
    scale = jnp.sum(jnp.where(lane == j, weight[...], 0.0), axis=1, keepdims=True)
    g = jnp.dot(x[...], gate[0], preferred_element_type=jnp.float32)
    u = jnp.dot(x[...], up[0], preferred_element_type=jnp.float32)
    out[...] = (g / (1.0 + jnp.exp(-g)) * u * scale).astype(out.dtype)


def reduce_kernel(
    n_z, n_t, n_d, chunk, act, wd_hbm, out,
    wd, keep, core_out, core_in, half_out, half_in, own, chip_out, chip_in,
    wd_sem, c_send, c_recv, x_send, x_recv, z_send, z_recv,
):
    z, t, d = lax.axis_index("expert"), lax.axis_index("tensor"), lax.axis_index("dp")
    rows, width = out.shape
    per_half = width // chunk
    steps = n_t * per_half
    group = n_z * rows

    def half_of(s):
        return lax.rem(t + 1 + lax.rem(s, n_t), n_t)

    def load(s):
        column = pl.multiple_of(half_of(s) * width + (s // n_t) * chunk, chunk)
        return pltpu.make_async_copy(
            wd_hbm.at[:, pl.ds(column, chunk)], wd.at[s], wd_sem.at[s]
        )

    def core_copy(s):
        return pltpu.make_async_remote_copy(
            core_out.at[s], core_in.at[s], c_send.at[s], c_recv.at[s],
            device_id={"dp": 1 - d}, device_id_type=MESH,
        )

    def half_copy(s):
        h = lax.rem(s, n_t) + 1
        k = s // n_t
        return pltpu.make_async_remote_copy(
            half_out.at[h - 1, k], half_in.at[h - 1, k], x_send.at[h, k], x_recv.at[h, k],
            device_id={"tensor": lax.rem(t + h, n_t)}, device_id_type=MESH,
        )

    def chip_copy(i, k):
        target = lax.rem(z + i, n_z)
        return pltpu.make_async_remote_copy(
            chip_out.at[k, pl.ds(pl.multiple_of(target * rows, rows), rows)],
            chip_in.at[i, k], z_send.at[i, k], z_recv.at[i, k],
            device_id={"expert": target}, device_id_type=MESH,
        )

    for s in range(steps):
        load(s).start()
    greet(z, t, d, n_z, n_t, n_d, False)

    def core_arrival(s):
        core_copy(s).wait_recv()
        total = keep[lax.rem(s, 2)] + core_in[s].astype(jnp.float32)
        k = s // n_t

        @pl.when(lax.rem(s, n_t) != n_t - 1)
        def _():
            half_out[lax.rem(s, n_t), k] = total.astype(jnp.bfloat16)
            half_copy(s).start()

        @pl.when(lax.rem(s, n_t) == n_t - 1)
        def _():
            own[k] = total

    @pl.loop(0, steps)
    def _(s):
        load(s).wait()
        core_out[s] = jnp.dot(
            act[pl.ds(pl.multiple_of((1 - d) * group, group), group), :], wd[s],
            preferred_element_type=jnp.float32,
        ).astype(jnp.bfloat16)
        core_copy(s).start()
        keep[lax.rem(s, 2)] = jnp.dot(
            act[pl.ds(pl.multiple_of(d * group, group), group), :], wd[s],
            preferred_element_type=jnp.float32,
        )

        @pl.when(s > 0)
        def _():
            core_arrival(s - 1)

    core_arrival(steps - 1)

    @pl.loop(0, per_half)
    def _(k):
        total = own[k]
        for h in range(1, n_t):
            half_copy(k * n_t + h - 1).wait_recv()
            total = total + half_in[h - 1, k].astype(jnp.float32)
        own[k] = total
        chip_out[k] = total.astype(jnp.bfloat16)
        for i in range(1, n_z):
            chip_copy(i, k).start()

    @pl.loop(0, per_half)
    def _(k):
        total = own[k, pl.ds(pl.multiple_of(z * rows, rows), rows), :]
        for i in range(1, n_z):
            chip_copy(i, k).wait_recv()
            total = total + chip_in[i, k].astype(jnp.float32)
        out[:, pl.ds(pl.multiple_of(k * chunk, chunk), chunk)] = total.astype(out.dtype)

    @pl.loop(0, steps)
    def _(s):
        core_copy(s).wait_send()

        @pl.when(lax.rem(s, n_t) != n_t - 1)
        def _():
            half_copy(s).wait_send()

    @pl.loop(0, per_half)
    def _(k):
        for i in range(1, n_z):
            chip_copy(i, k).wait_send()


def on_device(
    attn, o_weight, residual, norm_gain, expert_ids, route_weights, w_gate, w_up, w_down
):
    n_z, n_t, n_d = lax.axis_size("expert"), lax.axis_size("tensor"), lax.axis_size("dp")
    z, d = lax.axis_index("expert"), lax.axis_index("dp")
    rows, depth = attn.shape
    width = residual.shape[1]
    full = norm_gain.shape[0]
    mine, _, hidden_units = w_gate.shape
    experts = mine * n_z * n_d
    all_rows = rows * n_z * n_d
    held = o_weight.shape[1]
    dma, vmem, bf16, f32 = pltpu.SemaphoreType.DMA, pltpu.VMEM, jnp.bfloat16, jnp.float32
    in_vmem = pl.BlockSpec(memory_space=pltpu.VMEM)
    in_any = pl.BlockSpec(memory_space=pl.ANY)

    named = expert_ids[:, :, None] == jnp.arange(experts, dtype=jnp.int32)
    weight_map = jnp.sum(jnp.where(named, route_weights[:, :, None], 0.0), axis=1)
    weight_map = lax.all_gather(weight_map, ("expert", "dp"), axis=0, tiled=True)
    weight_map = weight_map.reshape(n_z, n_d, rows, experts).transpose(1, 0, 2, 3)
    weight_map = lax.dynamic_slice_in_dim(
        weight_map.reshape(all_rows, experts), (z * n_d + d) * mine, mine, 1
    )

    x = pl.pallas_call(
        functools.partial(gather_kernel, n_z, n_t, n_d),
        out_shape=jax.ShapeDtypeStruct((all_rows, full), bf16),
        in_specs=[in_vmem, in_any, in_vmem, in_vmem],
        out_specs=in_vmem,
        scratch_shapes=[
            vmem((n_d * rows, depth), bf16),
            vmem((depth, held), bf16),
            vmem((n_d * rows, held), bf16),
            vmem((n_t, rows, width), bf16),
            vmem((n_t, rows, 128), f32),
            dma,
            dma((n_d,)), dma((n_d,)),
            dma((held // width, n_d)), dma((n_t,)),
            dma((n_t,)), dma((n_t,)),
            dma((n_z,)), dma((n_z,)),
            dma((n_t, n_z)), dma((n_t, n_z)),
            dma((n_d, n_t, n_z)), dma((n_d, n_t, n_z)),
        ],
        compiler_params=pltpu.CompilerParams(
            collective_id=0, has_side_effects=True, vmem_limit_bytes=40 * MIB
        ),
        name="project_gather",
    )(attn, o_weight, residual, norm_gain.reshape(1, full))

    tile = min(256, hidden_units)
    tiles = hidden_units // tile
    act = pl.pallas_call(
        experts_kernel,
        grid=(mine, tiles),
        out_shape=jax.ShapeDtypeStruct((all_rows, mine * hidden_units), bf16),
        in_specs=[
            pl.BlockSpec((all_rows, full), lambda j, i: (0, 0)),
            pl.BlockSpec((1, full, tile), lambda j, i: (j, 0, i)),
            pl.BlockSpec((1, full, tile), lambda j, i: (j, 0, i)),
            pl.BlockSpec((all_rows, mine), lambda j, i: (0, 0)),
        ],
        out_specs=pl.BlockSpec((all_rows, tile), lambda j, i: (0, j * tiles + i)),
        compiler_params=pltpu.CompilerParams(vmem_limit_bytes=56 * MIB),
        name="gate_up",
    )(x, w_gate, w_up, weight_map)

    chunk = min(512, width)
    per_half = width // chunk
    steps = n_t * per_half
    group = n_z * rows
    return pl.pallas_call(
        functools.partial(reduce_kernel, n_z, n_t, n_d, chunk),
        out_shape=jax.ShapeDtypeStruct((rows, width), bf16),
        in_specs=[in_vmem, in_any],
        out_specs=in_vmem,
        scratch_shapes=[
            vmem((steps, mine * hidden_units, chunk), bf16),
            vmem((2, group, chunk), f32),
            vmem((steps, group, chunk), bf16),
            vmem((steps, group, chunk), bf16),
            vmem((n_t - 1, per_half, group, chunk), bf16),
            vmem((n_t - 1, per_half, group, chunk), bf16),
            vmem((per_half, group, chunk), f32),
            vmem((per_half, group, chunk), bf16),
            vmem((n_z, per_half, rows, chunk), bf16),
            dma((steps,)),
            dma((steps,)), dma((steps,)),
            dma((n_t, per_half)), dma((n_t, per_half)),
            dma((n_z, per_half)), dma((n_z, per_half)),
        ],
        compiler_params=pltpu.CompilerParams(
            collective_id=1, has_side_effects=True, vmem_limit_bytes=56 * MIB
        ),
        name="down_reduce",
    )(act, w_down.reshape(mine * hidden_units, full))


def solution(mesh):
    rows = ("groups", "expert", "dp")
    return jax.shard_map(
        on_device,
        mesh=mesh,
        in_specs=(
            P(rows, "tensor"),
            P("tensor", "dp"),
            P(rows, "tensor"),
            P(),
            P(rows, None),
            P(rows, None),
            P(("expert", "dp"), None, "tensor"),
            P(("expert", "dp"), None, "tensor"),
            P(("expert", "dp"), "tensor", None),
        ),
        out_specs=P(rows, "tensor"),
        check_vma=False,
    )
```

```python
import functools

import jax
import jax.numpy as jnp
from jax import lax
from jax.experimental import pallas as pl
from jax.experimental.pallas import tpu as pltpu
from jax.sharding import PartitionSpec as P

MESH = pl.DeviceIdType.MESH
epsilon = 1e-06
MIB = 1 << 20


def greet(z, t, d, n_z, n_t, n_d, square):
    barrier = pltpu.get_barrier_semaphore()
    count = 0
    for i in range(n_t):
        for j in range(n_d):
            if (i or j) and (square or not (i and j)):
                pl.semaphore_signal(
                    barrier,
                    inc=1,
                    device_id={"tensor": lax.rem(t + i, n_t), "dp": lax.rem(d + j, n_d)},
                    device_id_type=MESH,
                )
                count += 1
    for i in range(1, n_z):
        pl.semaphore_signal(
            barrier, inc=1, device_id={"expert": lax.rem(z + i, n_z)}, device_id_type=MESH
        )
        count += 1
    pl.semaphore_wait(barrier, count)


def gather_kernel(
    n_z, n_t, n_d, attn_hbm, ow_hbm, residual_hbm, gain, routes, out, all_routes,
    pair, residual, ow, part, landed, squares,
    ow_sem, in_sem, m_send, m_recv, n_send, n_recv, a_send, a_recv, p_send, p_recv, s_send, s_recv,
    z_send, z_recv, x_send, x_recv, c_send, c_recv,
):
    z, t, d = lax.axis_index("expert"), lax.axis_index("tensor"), lax.axis_index("dp")
    rows, width = residual.shape
    held = ow.shape[1]
    blocks = held // width
    attn = pair.at[pl.ds(pl.multiple_of(d * rows, rows), rows), :]
    load_attn = pltpu.make_async_copy(attn_hbm, attn, in_sem.at[0])
    load_attn.start()
    load_residual = pltpu.make_async_copy(residual_hbm, residual, in_sem.at[1])
    load_residual.start()
    load = pltpu.make_async_copy(ow_hbm, ow, ow_sem)
    load.start()
    greet(z, t, d, n_z, n_t, n_d, True)

    load_attn.wait()
    sent = []
    for j in range(1, n_d):
        copy = pltpu.make_async_remote_copy(
            attn, attn, a_send.at[j], a_recv.at[j],
            device_id={"dp": lax.rem(d + j, n_d)}, device_id_type=MESH,
        )
        copy.start()
        sent.append(copy)
    def routes_of(core, chip):
        first = pl.multiple_of((core * n_z + chip) * rows, rows)
        return all_routes.at[pl.ds(first, rows), :]

    routes_of(d, z)[...] = routes[...]
    maps = []
    for i in range(1, n_z):
        copy = pltpu.make_async_remote_copy(
            routes, routes_of(d, z), m_send.at[i], m_recv.at[i],
            device_id={"expert": lax.rem(z + i, n_z)}, device_id_type=MESH,
        )
        copy.start()
        maps.append(copy)

    load.wait()
    for copy in sent:
        copy.wait()

    tile = min(512, width)
    for first in range(0, held, tile):
        part[:, pl.ds(first, tile)] = jnp.dot(
            pair[...], ow[:, pl.ds(first, tile)], preferred_element_type=jnp.float32
        ).astype(jnp.bfloat16)

    def piece(i, j):
        owner, core = d * blocks + i, lax.rem(d + j, n_d)
        source = part.at[pl.ds(core * rows, rows), pl.ds(i * width, width)]
        copy = pltpu.make_async_remote_copy(
            source, landed.at[t], p_send.at[i, j], p_recv.at[t],
            device_id={"tensor": owner, "dp": core}, device_id_type=MESH,
        )
        return owner, core, copy

    for i in range(blocks):
        for j in range(n_d):
            owner, core, copy = piece(i, j)
            if j:
                copy.start()
            else:
                @pl.when(owner != t)
                def _():
                    copy.start()

                @pl.when(owner == t)
                def _():
                    landed[t] = part[pl.ds(d * rows, rows), pl.ds(i * width, width)]

    for i in range(n_t):
        arrival = pltpu.make_async_remote_copy(
            landed.at[i], landed.at[i], p_send.at[0, 0], p_recv.at[i],
            device_id={"tensor": i}, device_id_type=MESH,
        )

        @pl.when(jnp.logical_or(i != t, t // blocks != d))
        def _():
            arrival.wait_recv()

    load_residual.wait()
    hidden = residual[...].astype(jnp.float32)
    for i in range(n_t):
        hidden = hidden + landed[i].astype(jnp.float32)
    hidden = hidden.astype(jnp.bfloat16).astype(jnp.float32)
    squares[0] = jnp.broadcast_to(
        jnp.sum(hidden * hidden, axis=1, keepdims=True), squares.shape[1:]
    )
    sums = []
    for i in range(1, n_t):
        copy = pltpu.make_async_remote_copy(
            squares.at[0], squares.at[i], s_send.at[i], s_recv.at[i],
            device_id={"tensor": lax.rem(t + i, n_t)}, device_id_type=MESH,
        )
        copy.start()
        sums.append(copy)
    for copy in sums:
        copy.wait()
    total = squares[0]
    for i in range(1, n_t):
        total = total + squares[i]
    inverse = lax.rsqrt(total[:, :1] / (width * n_t) + epsilon)
    columns = pl.ds(pl.multiple_of(t * width, width), width)
    normed = hidden * inverse * gain[:, columns].astype(jnp.float32)

    def block(core, chip, half):
        return out.at[
            pl.ds(pl.multiple_of((core * n_z + chip) * rows, rows), rows),
            pl.ds(pl.multiple_of(half * width, width), width),
        ]

    block(d, z, t)[...] = normed.astype(jnp.bfloat16)

    started = []

    def to_tensor(i, chip):
        copies = []
        for h in range(1, n_t):
            ref = block(d, lax.rem(z - chip + n_z, n_z), t)
            copy = pltpu.make_async_remote_copy(
                ref, ref, x_send.at[h, chip], x_recv.at[h, chip],
                device_id={"tensor": lax.rem(t + h, n_t)}, device_id_type=MESH,
            )
            copy.start()
            copies.append(copy)
        started.extend(copies)

    def to_core(h, chip):
        for j in range(1, n_d):
            ref = block(d, lax.rem(z - chip + n_z, n_z), lax.rem(t - h + n_t, n_t))
            copy = pltpu.make_async_remote_copy(
                ref, ref, c_send.at[j, h, chip], c_recv.at[j, h, chip],
                device_id={"dp": lax.rem(d + j, n_d)}, device_id_type=MESH,
            )
            copy.start()
            started.append(copy)

    to_tensor(t, 0)
    order = sorted(range(1, n_z), key=lambda i: min(i, n_z - i))
    for i in order:
        ref = block(d, z, t)
        copy = pltpu.make_async_remote_copy(
            ref, ref, z_send.at[i], z_recv.at[i],
            device_id={"expert": lax.rem(z + i, n_z)}, device_id_type=MESH,
        )
        copy.start()
        started.append(copy)
    to_core(0, 0)
    for i, copy in enumerate(maps):
        copy.wait_send()
        ref = routes_of(d, lax.rem(z - i - 1 + n_z, n_z))
        pltpu.make_async_remote_copy(
            ref, ref, m_send.at[i + 1], m_recv.at[i + 1],
            device_id={"tensor": t}, device_id_type=MESH,
        ).wait_recv()
    turned = []
    for j in range(1, n_d):
        ref = all_routes.at[pl.ds(pl.multiple_of(d * n_z * rows, rows), n_z * rows), :]
        copy = pltpu.make_async_remote_copy(
            ref, ref, n_send.at[j], n_recv.at[j],
            device_id={"dp": lax.rem(d + j, n_d)}, device_id_type=MESH,
        )
        copy.start()
        turned.append(copy)

    def await_block(ref, sem):
        pltpu.make_async_remote_copy(
            ref, ref, z_send.at[0], sem, device_id={"tensor": t}, device_id_type=MESH
        ).wait_recv()

    def from_tensor(chip):
        for h in range(1, n_t):
            await_block(
                block(d, lax.rem(z - chip + n_z, n_z), lax.rem(t - h + n_t, n_t)),
                x_recv.at[h, chip],
            )
            to_core(h, chip)

    for i in order:
        await_block(block(d, lax.rem(z - i + n_z, n_z), t), z_recv.at[i])
        to_tensor(t, i)
        to_core(0, i)
    for i in [0] + order:
        from_tensor(i)
    for i in [0] + order:
        for h in range(n_t):
            for j in range(1, n_d):
                await_block(
                    block(
                        lax.rem(d - j + n_d, n_d),
                        lax.rem(z - i + n_z, n_z),
                        lax.rem(t - h + n_t, n_t),
                    ),
                    c_recv.at[j, h, i],
                )
    for copy in turned:
        copy.wait()
    for copy in started:
        copy.wait_send()
    for i in range(blocks):
        for j in range(n_d):
            owner, core, copy = piece(i, j)
            if j:
                copy.wait_send()
            else:
                @pl.when(owner != t)
                def _():
                    copy.wait_send()


def experts_kernel(n_d, mine, x, gate, up, weight, out):
    j = pl.program_id(0)
    first = (lax.axis_index("expert") * n_d + lax.axis_index("dp")) * mine
    lane = lax.broadcasted_iota(jnp.int32, weight.shape, 1)
    scale = jnp.sum(jnp.where(lane == first + j, weight[...], 0.0), axis=1, keepdims=True)
    g = jnp.dot(x[...], gate[0], preferred_element_type=jnp.float32)
    u = jnp.dot(x[...], up[0], preferred_element_type=jnp.float32)
    out[...] = (g / (1.0 + jnp.exp(-g)) * u * scale).astype(out.dtype)


def reduce_kernel(
    n_z, n_t, n_d, chunk, act, wd_hbm, out,
    wd, keep, core_out, core_in, half_out, half_in, own, chip_out, chip_in,
    wd_sem, c_send, c_recv, x_send, x_recv, z_send, z_recv,
):
    z, t, d = lax.axis_index("expert"), lax.axis_index("tensor"), lax.axis_index("dp")
    rows, width = out.shape
    per_half = width // chunk
    steps = n_t * per_half
    group = n_z * rows

    def half_of(s):
        return lax.rem(t + 1 + lax.rem(s, n_t), n_t)

    def load(s):
        column = pl.multiple_of(half_of(s) * width + (s // n_t) * chunk, chunk)
        return pltpu.make_async_copy(
            wd_hbm.at[:, pl.ds(column, chunk)], wd.at[s], wd_sem.at[s]
        )

    def core_copy(s):
        return pltpu.make_async_remote_copy(
            core_out.at[s], core_in.at[s], c_send.at[s], c_recv.at[s],
            device_id={"dp": 1 - d}, device_id_type=MESH,
        )

    def half_copy(s):
        h = lax.rem(s, n_t) + 1
        k = s // n_t
        return pltpu.make_async_remote_copy(
            half_out.at[h - 1, k], half_in.at[h - 1, k], x_send.at[h, k], x_recv.at[h, k],
            device_id={"tensor": lax.rem(t + h, n_t)}, device_id_type=MESH,
        )

    def chip_copy(i, k):
        target = lax.rem(z + i, n_z)
        return pltpu.make_async_remote_copy(
            chip_out.at[k, pl.ds(pl.multiple_of(target * rows, rows), rows)],
            chip_in.at[i, k], z_send.at[i, k], z_recv.at[i, k],
            device_id={"expert": target}, device_id_type=MESH,
        )

    for s in range(steps):
        load(s).start()
    greet(z, t, d, n_z, n_t, n_d, False)

    def core_arrival(s):
        core_copy(s).wait_recv()
        total = keep[lax.rem(s, 2)] + core_in[s].astype(jnp.float32)
        k = s // n_t

        @pl.when(lax.rem(s, n_t) != n_t - 1)
        def _():
            half_out[lax.rem(s, n_t), k] = total.astype(jnp.bfloat16)
            half_copy(s).start()

        @pl.when(lax.rem(s, n_t) == n_t - 1)
        def _():
            own[k] = total

    @pl.loop(0, steps)
    def _(s):
        load(s).wait()
        core_out[s] = jnp.dot(
            act[pl.ds(pl.multiple_of((1 - d) * group, group), group), :], wd[s],
            preferred_element_type=jnp.float32,
        ).astype(jnp.bfloat16)
        core_copy(s).start()
        keep[lax.rem(s, 2)] = jnp.dot(
            act[pl.ds(pl.multiple_of(d * group, group), group), :], wd[s],
            preferred_element_type=jnp.float32,
        )

        @pl.when(s > 0)
        def _():
            core_arrival(s - 1)

    core_arrival(steps - 1)

    @pl.loop(0, per_half)
    def _(k):
        total = own[k]
        for h in range(1, n_t):
            half_copy(k * n_t + h - 1).wait_recv()
            total = total + half_in[h - 1, k].astype(jnp.float32)
        own[k] = total
        chip_out[k] = total.astype(jnp.bfloat16)
        for i in range(1, n_z):
            chip_copy(i, k).start()

    @pl.loop(0, per_half)
    def _(k):
        total = own[k, pl.ds(pl.multiple_of(z * rows, rows), rows), :]
        for i in range(1, n_z):
            chip_copy(i, k).wait_recv()
            total = total + chip_in[i, k].astype(jnp.float32)
        out[:, pl.ds(pl.multiple_of(k * chunk, chunk), chunk)] = total.astype(out.dtype)

    @pl.loop(0, steps)
    def _(s):
        core_copy(s).wait_send()

        @pl.when(lax.rem(s, n_t) != n_t - 1)
        def _():
            half_copy(s).wait_send()

    @pl.loop(0, per_half)
    def _(k):
        for i in range(1, n_z):
            chip_copy(i, k).wait_send()


def on_device(
    attn, o_weight, residual, norm_gain, expert_ids, route_weights, w_gate, w_up, w_down
):
    n_z, n_t, n_d = lax.axis_size("expert"), lax.axis_size("tensor"), lax.axis_size("dp")
    rows, depth = attn.shape
    width = residual.shape[1]
    full = norm_gain.shape[0]
    mine, _, hidden_units = w_gate.shape
    experts = mine * n_z * n_d
    all_rows = rows * n_z * n_d
    held = o_weight.shape[1]
    dma, vmem, bf16, f32 = pltpu.SemaphoreType.DMA, pltpu.VMEM, jnp.bfloat16, jnp.float32
    in_vmem = pl.BlockSpec(memory_space=pltpu.VMEM)
    in_any = pl.BlockSpec(memory_space=pl.ANY)

    named = expert_ids[:, :, None] == jnp.arange(experts, dtype=jnp.int32)
    weight_map = jnp.sum(jnp.where(named, route_weights[:, :, None], 0.0), axis=1)
    lanes = -(-experts // 128) * 128
    weight_map = jnp.pad(weight_map, ((0, 0), (0, lanes - experts)))

    x, weight_map = pl.pallas_call(
        functools.partial(gather_kernel, n_z, n_t, n_d),
        out_shape=[
            jax.ShapeDtypeStruct((all_rows, full), bf16),
            jax.ShapeDtypeStruct((all_rows, lanes), f32),
        ],
        in_specs=[in_any, in_any, in_any, in_vmem, in_vmem],
        out_specs=[in_vmem, in_vmem],
        scratch_shapes=[
            vmem((n_d * rows, depth), bf16),
            vmem((rows, width), bf16),
            vmem((depth, held), bf16),
            vmem((n_d * rows, held), bf16),
            vmem((n_t, rows, width), bf16),
            vmem((n_t, rows, 128), f32),
            dma, dma((2,)),
            dma((n_z,)), dma((n_z,)), dma((n_d,)), dma((n_d,)),
            dma((n_d,)), dma((n_d,)),
            dma((held // width, n_d)), dma((n_t,)),
            dma((n_t,)), dma((n_t,)),
            dma((n_z,)), dma((n_z,)),
            dma((n_t, n_z)), dma((n_t, n_z)),
            dma((n_d, n_t, n_z)), dma((n_d, n_t, n_z)),
        ],
        compiler_params=pltpu.CompilerParams(
            collective_id=0, has_side_effects=True, vmem_limit_bytes=60 * MIB
        ),
        name="project_gather",
    )(attn, o_weight, residual, norm_gain.reshape(1, full), weight_map)

    tile = min(256, hidden_units)
    tiles = hidden_units // tile
    act = pl.pallas_call(
        functools.partial(experts_kernel, n_d, mine),
        grid=(mine, tiles),
        out_shape=jax.ShapeDtypeStruct((all_rows, mine * hidden_units), bf16),
        in_specs=[
            pl.BlockSpec((all_rows, full), lambda j, i: (0, 0)),
            pl.BlockSpec((1, full, tile), lambda j, i: (j, 0, i)),
            pl.BlockSpec((1, full, tile), lambda j, i: (j, 0, i)),
            pl.BlockSpec((all_rows, lanes), lambda j, i: (0, 0)),
        ],
        out_specs=pl.BlockSpec((all_rows, tile), lambda j, i: (0, j * tiles + i)),
        compiler_params=pltpu.CompilerParams(vmem_limit_bytes=56 * MIB),
        name="gate_up",
    )(x, w_gate, w_up, weight_map)

    chunk = min(512, width)
    per_half = width // chunk
    steps = n_t * per_half
    group = n_z * rows
    return pl.pallas_call(
        functools.partial(reduce_kernel, n_z, n_t, n_d, chunk),
        out_shape=jax.ShapeDtypeStruct((rows, width), bf16),
        in_specs=[in_vmem, in_any],
        out_specs=in_vmem,
        scratch_shapes=[
            vmem((steps, mine * hidden_units, chunk), bf16),
            vmem((2, group, chunk), f32),
            vmem((steps, group, chunk), bf16),
            vmem((steps, group, chunk), bf16),
            vmem((n_t - 1, per_half, group, chunk), bf16),
            vmem((n_t - 1, per_half, group, chunk), bf16),
            vmem((per_half, group, chunk), f32),
            vmem((per_half, group, chunk), bf16),
            vmem((n_z, per_half, rows, chunk), bf16),
            dma((steps,)),
            dma((steps,)), dma((steps,)),
            dma((n_t, per_half)), dma((n_t, per_half)),
            dma((n_z, per_half)), dma((n_z, per_half)),
        ],
        compiler_params=pltpu.CompilerParams(
            collective_id=1, has_side_effects=True, vmem_limit_bytes=56 * MIB
        ),
        name="down_reduce",
    )(act, w_down.reshape(mine * hidden_units, full))


def solution(mesh):
    rows = ("groups", "expert", "dp")
    return jax.shard_map(
        on_device,
        mesh=mesh,
        in_specs=(
            P(rows, "tensor"),
            P("tensor", "dp"),
            P(rows, "tensor"),
            P(),
            P(rows, None),
            P(rows, None),
            P(("expert", "dp"), None, "tensor"),
            P(("expert", "dp"), None, "tensor"),
            P(("expert", "dp"), "tensor", None),
        ),
        out_specs=P(rows, "tensor"),
        check_vma=False,
    )
```

```python
import functools

import jax
import jax.numpy as jnp
from jax import lax
from jax.experimental import pallas as pl
from jax.experimental.pallas import tpu as pltpu
from jax.sharding import PartitionSpec as P

MESH = pl.DeviceIdType.MESH
epsilon = 1e-06
MIB = 1 << 20


def greet(z, t, d, n_z, n_t, n_d, square):
    barrier = pltpu.get_barrier_semaphore()
    count = 0
    for i in range(n_t):
        for j in range(n_d):
            if (i or j) and (square or not (i and j)):
                pl.semaphore_signal(
                    barrier,
                    inc=1,
                    device_id={"tensor": lax.rem(t + i, n_t), "dp": lax.rem(d + j, n_d)},
                    device_id_type=MESH,
                )
                count += 1
    for i in range(1, n_z):
        pl.semaphore_signal(
            barrier, inc=1, device_id={"expert": lax.rem(z + i, n_z)}, device_id_type=MESH
        )
        count += 1
    pl.semaphore_wait(barrier, count)


def gather_kernel(
    n_z, n_t, n_d, attn_hbm, ow_hbm, residual_hbm, gain, routes, gate_hbm, up_hbm, act,
    out, all_routes, tiles, sums_of, tile_sem, pair, residual, ow, part, landed, squares,
    ow_sem, in_sem, m_send, m_recv, n_send, n_recv, a_send, a_recv, p_send, p_recv, s_send, s_recv,
    z_send, z_recv, x_send, x_recv, c_send, c_recv,
):
    z, t, d = lax.axis_index("expert"), lax.axis_index("tensor"), lax.axis_index("dp")
    rows, width = residual.shape
    held = ow.shape[1]
    blocks = held // width
    attn = pair.at[pl.ds(pl.multiple_of(d * rows, rows), rows), :]
    load_attn = pltpu.make_async_copy(attn_hbm, attn, in_sem.at[0])
    load_attn.start()
    load_residual = pltpu.make_async_copy(residual_hbm, residual, in_sem.at[1])
    load_residual.start()
    load = pltpu.make_async_copy(ow_hbm, ow, ow_sem)
    load.start()
    mine, _, units = gate_hbm.shape
    slots = tiles.shape[0]
    count = 2 * mine * n_t

    def load_tile(n):
        h, j = n // (2 * mine), n % (2 * mine) // 2
        first = pl.multiple_of(lax.rem(t - h + n_t, n_t) * width, width)
        source = (up_hbm if n % 2 else gate_hbm).at[j, pl.ds(first, width), :]
        return pltpu.make_async_copy(source, tiles.at[n % slots], tile_sem.at[n % slots])

    for n in range(min(slots, count)):
        load_tile(n).start()
    greet(z, t, d, n_z, n_t, n_d, True)

    load_attn.wait()
    sent = []
    for j in range(1, n_d):
        copy = pltpu.make_async_remote_copy(
            attn, attn, a_send.at[j], a_recv.at[j],
            device_id={"dp": lax.rem(d + j, n_d)}, device_id_type=MESH,
        )
        copy.start()
        sent.append(copy)
    def routes_of(core, chip):
        first = pl.multiple_of((core * n_z + chip) * rows, rows)
        return all_routes.at[pl.ds(first, rows), :]

    routes_of(d, z)[...] = routes[...]
    maps = []
    for i in range(1, n_z):
        copy = pltpu.make_async_remote_copy(
            routes, routes_of(d, z), m_send.at[i], m_recv.at[i],
            device_id={"expert": lax.rem(z + i, n_z)}, device_id_type=MESH,
        )
        copy.start()
        maps.append(copy)

    load.wait()
    for copy in sent:
        copy.wait()

    tile = min(512, width)
    for first in range(0, held, tile):
        part[:, pl.ds(first, tile)] = jnp.dot(
            pair[...], ow[:, pl.ds(first, tile)], preferred_element_type=jnp.float32
        ).astype(jnp.bfloat16)

    def piece(i, j):
        owner, core = d * blocks + i, lax.rem(d + j, n_d)
        source = part.at[pl.ds(core * rows, rows), pl.ds(i * width, width)]
        copy = pltpu.make_async_remote_copy(
            source, landed.at[t], p_send.at[i, j], p_recv.at[t],
            device_id={"tensor": owner, "dp": core}, device_id_type=MESH,
        )
        return owner, core, copy

    for i in range(blocks):
        for j in range(n_d):
            owner, core, copy = piece(i, j)
            if j:
                copy.start()
            else:
                @pl.when(owner != t)
                def _():
                    copy.start()

                @pl.when(owner == t)
                def _():
                    landed[t] = part[pl.ds(d * rows, rows), pl.ds(i * width, width)]

    for i in range(n_t):
        arrival = pltpu.make_async_remote_copy(
            landed.at[i], landed.at[i], p_send.at[0, 0], p_recv.at[i],
            device_id={"tensor": i}, device_id_type=MESH,
        )

        @pl.when(jnp.logical_or(i != t, t // blocks != d))
        def _():
            arrival.wait_recv()

    load_residual.wait()
    hidden = residual[...].astype(jnp.float32)
    for i in range(n_t):
        hidden = hidden + landed[i].astype(jnp.float32)
    hidden = hidden.astype(jnp.bfloat16).astype(jnp.float32)
    squares[0] = jnp.broadcast_to(
        jnp.sum(hidden * hidden, axis=1, keepdims=True), squares.shape[1:]
    )
    sums = []
    for i in range(1, n_t):
        copy = pltpu.make_async_remote_copy(
            squares.at[0], squares.at[i], s_send.at[i], s_recv.at[i],
            device_id={"tensor": lax.rem(t + i, n_t)}, device_id_type=MESH,
        )
        copy.start()
        sums.append(copy)
    for copy in sums:
        copy.wait()
    total = squares[0]
    for i in range(1, n_t):
        total = total + squares[i]
    inverse = lax.rsqrt(total[:, :1] / (width * n_t) + epsilon)
    columns = pl.ds(pl.multiple_of(t * width, width), width)
    normed = hidden * inverse * gain[:, columns].astype(jnp.float32)

    def block(core, chip, half):
        return out.at[
            pl.ds(pl.multiple_of((core * n_z + chip) * rows, rows), rows),
            pl.ds(pl.multiple_of(half * width, width), width),
        ]

    block(d, z, t)[...] = normed.astype(jnp.bfloat16)

    started = []

    def to_tensor(i, chip):
        copies = []
        for h in range(1, n_t):
            ref = block(d, lax.rem(z - chip + n_z, n_z), t)
            copy = pltpu.make_async_remote_copy(
                ref, ref, x_send.at[h, chip], x_recv.at[h, chip],
                device_id={"tensor": lax.rem(t + h, n_t)}, device_id_type=MESH,
            )
            copy.start()
            copies.append(copy)
        started.extend(copies)

    def to_core(h, chip):
        for j in range(1, n_d):
            ref = block(d, lax.rem(z - chip + n_z, n_z), lax.rem(t - h + n_t, n_t))
            copy = pltpu.make_async_remote_copy(
                ref, ref, c_send.at[j, h, chip], c_recv.at[j, h, chip],
                device_id={"dp": lax.rem(d + j, n_d)}, device_id_type=MESH,
            )
            copy.start()
            started.append(copy)

    to_tensor(t, 0)
    order = sorted(range(1, n_z), key=lambda i: min(i, n_z - i))
    for i in order:
        ref = block(d, z, t)
        copy = pltpu.make_async_remote_copy(
            ref, ref, z_send.at[i], z_recv.at[i],
            device_id={"expert": lax.rem(z + i, n_z)}, device_id_type=MESH,
        )
        copy.start()
        started.append(copy)
    to_core(0, 0)
    for i, copy in enumerate(maps):
        copy.wait_send()
        ref = routes_of(d, lax.rem(z - i - 1 + n_z, n_z))
        pltpu.make_async_remote_copy(
            ref, ref, m_send.at[i + 1], m_recv.at[i + 1],
            device_id={"tensor": t}, device_id_type=MESH,
        ).wait_recv()
    turned = []
    for j in range(1, n_d):
        ref = all_routes.at[pl.ds(pl.multiple_of(d * n_z * rows, rows), n_z * rows), :]
        copy = pltpu.make_async_remote_copy(
            ref, ref, n_send.at[j], n_recv.at[j],
            device_id={"dp": lax.rem(d + j, n_d)}, device_id_type=MESH,
        )
        copy.start()
        turned.append(copy)

    def await_block(ref, sem):
        pltpu.make_async_remote_copy(
            ref, ref, z_send.at[0], sem, device_id={"tensor": t}, device_id_type=MESH
        ).wait_recv()

    def from_tensor(chip):
        for h in range(1, n_t):
            await_block(
                block(d, lax.rem(z - chip + n_z, n_z), lax.rem(t - h + n_t, n_t)),
                x_recv.at[h, chip],
            )
            to_core(h, chip)

    for i in order:
        await_block(block(d, lax.rem(z - i + n_z, n_z), t), z_recv.at[i])
        to_tensor(t, i)
        to_core(0, i)
    def await_core(h):
        for i in [0] + order:
            for j in range(1, n_d):
                await_block(
                    block(
                        lax.rem(d - j + n_d, n_d),
                        lax.rem(z - i + n_z, n_z),
                        lax.rem(t - h + n_t, n_t),
                    ),
                    c_recv.at[j, h, i],
                )

    step = min(256, units)
    lane = lax.broadcasted_iota(jnp.int32, all_routes.shape, 1)
    base = (z * n_d + d) * mine

    def product(h, j):
        n = (h * mine + j) * 2
        load_tile(n).wait()
        load_tile(n + 1).wait()
        features = out.at[:, pl.ds(pl.multiple_of(lax.rem(t - h + n_t, n_t) * width, width), width)]
        if h == n_t - 1:
            scale = jnp.sum(jnp.where(lane == base + j, all_routes[...], 0.0), axis=1, keepdims=True)
        for first in range(0, units, step):
            cols = pl.ds(first, step)
            both = []
            for side in range(2):
                value = jnp.dot(
                    features[...], tiles[(n + side) % slots, :, cols],
                    preferred_element_type=jnp.float32,
                )
                if h:
                    value = value + sums_of[2 * j + side, :, cols]
                if h < n_t - 1:
                    sums_of[2 * j + side, :, cols] = value
                both.append(value)
            if h == n_t - 1:
                g, u = both
                act[:, pl.ds(j * units + first, step)] = (
                    g / (1.0 + jnp.exp(-g)) * u * scale
                ).astype(act.dtype)
        for later in (n + slots, n + 1 + slots):
            if later < count:
                load_tile(later).start()

    chips = [0] + order
    from_tensor(chips.pop(0))
    await_core(0)
    for copy in turned:
        copy.wait()
    for h in range(n_t):
        if h:
            await_core(h)
        for j in range(mine):
            product(h, j)
            if h == 0 and j < mine - 1 and chips:
                from_tensor(chips.pop(0))
        while chips:
            from_tensor(chips.pop(0))
    for copy in started:
        copy.wait_send()
    for i in range(blocks):
        for j in range(n_d):
            owner, core, copy = piece(i, j)
            if j:
                copy.wait_send()
            else:
                @pl.when(owner != t)
                def _():
                    copy.wait_send()


def reduce_kernel(
    n_z, n_t, n_d, chunk, act, wd_hbm, out,
    wd, keep, core_out, core_in, half_out, half_in, own, chip_out, chip_in,
    wd_sem, c_send, c_recv, x_send, x_recv, z_send, z_recv,
):
    z, t, d = lax.axis_index("expert"), lax.axis_index("tensor"), lax.axis_index("dp")
    rows, width = out.shape
    per_half = width // chunk
    steps = n_t * per_half
    group = n_z * rows

    def half_of(s):
        return lax.rem(t + 1 + lax.rem(s, n_t), n_t)

    def load(s):
        column = pl.multiple_of(half_of(s) * width + (s // n_t) * chunk, chunk)
        return pltpu.make_async_copy(
            wd_hbm.at[:, pl.ds(column, chunk)], wd.at[s], wd_sem.at[s]
        )

    def core_copy(s):
        return pltpu.make_async_remote_copy(
            core_out.at[s], core_in.at[s], c_send.at[s], c_recv.at[s],
            device_id={"dp": 1 - d}, device_id_type=MESH,
        )

    def half_copy(s):
        h = lax.rem(s, n_t) + 1
        k = s // n_t
        return pltpu.make_async_remote_copy(
            half_out.at[h - 1, k], half_in.at[h - 1, k], x_send.at[h, k], x_recv.at[h, k],
            device_id={"tensor": lax.rem(t + h, n_t)}, device_id_type=MESH,
        )

    def chip_copy(i, k):
        target = lax.rem(z + i, n_z)
        return pltpu.make_async_remote_copy(
            chip_out.at[k, pl.ds(pl.multiple_of(target * rows, rows), rows)],
            chip_in.at[i, k], z_send.at[i, k], z_recv.at[i, k],
            device_id={"expert": target}, device_id_type=MESH,
        )

    for s in range(steps):
        load(s).start()
    greet(z, t, d, n_z, n_t, n_d, False)

    def core_arrival(s):
        core_copy(s).wait_recv()
        total = keep[lax.rem(s, 2)] + core_in[s].astype(jnp.float32)
        k = s // n_t

        @pl.when(lax.rem(s, n_t) != n_t - 1)
        def _():
            half_out[lax.rem(s, n_t), k] = total.astype(jnp.bfloat16)
            half_copy(s).start()

        @pl.when(lax.rem(s, n_t) == n_t - 1)
        def _():
            own[k] = total

    @pl.loop(0, steps)
    def _(s):
        load(s).wait()
        core_out[s] = jnp.dot(
            act[pl.ds(pl.multiple_of((1 - d) * group, group), group), :], wd[s],
            preferred_element_type=jnp.float32,
        ).astype(jnp.bfloat16)
        core_copy(s).start()
        keep[lax.rem(s, 2)] = jnp.dot(
            act[pl.ds(pl.multiple_of(d * group, group), group), :], wd[s],
            preferred_element_type=jnp.float32,
        )

        @pl.when(s > 0)
        def _():
            core_arrival(s - 1)

    core_arrival(steps - 1)

    @pl.loop(0, per_half)
    def _(k):
        total = own[k]
        for h in range(1, n_t):
            half_copy(k * n_t + h - 1).wait_recv()
            total = total + half_in[h - 1, k].astype(jnp.float32)
        own[k] = total
        chip_out[k] = total.astype(jnp.bfloat16)
        for i in range(1, n_z):
            chip_copy(i, k).start()

    @pl.loop(0, per_half)
    def _(k):
        total = own[k, pl.ds(pl.multiple_of(z * rows, rows), rows), :]
        for i in range(1, n_z):
            chip_copy(i, k).wait_recv()
            total = total + chip_in[i, k].astype(jnp.float32)
        out[:, pl.ds(pl.multiple_of(k * chunk, chunk), chunk)] = total.astype(out.dtype)

    @pl.loop(0, steps)
    def _(s):
        core_copy(s).wait_send()

        @pl.when(lax.rem(s, n_t) != n_t - 1)
        def _():
            half_copy(s).wait_send()

    @pl.loop(0, per_half)
    def _(k):
        for i in range(1, n_z):
            chip_copy(i, k).wait_send()


def on_device(
    attn, o_weight, residual, norm_gain, expert_ids, route_weights, w_gate, w_up, w_down
):
    n_z, n_t, n_d = lax.axis_size("expert"), lax.axis_size("tensor"), lax.axis_size("dp")
    rows, depth = attn.shape
    width = residual.shape[1]
    full = norm_gain.shape[0]
    mine, _, hidden_units = w_gate.shape
    experts = mine * n_z * n_d
    all_rows = rows * n_z * n_d
    held = o_weight.shape[1]
    dma, vmem, bf16, f32 = pltpu.SemaphoreType.DMA, pltpu.VMEM, jnp.bfloat16, jnp.float32
    in_vmem = pl.BlockSpec(memory_space=pltpu.VMEM)
    in_any = pl.BlockSpec(memory_space=pl.ANY)

    named = expert_ids[:, :, None] == jnp.arange(experts, dtype=jnp.int32)
    weight_map = jnp.sum(jnp.where(named, route_weights[:, :, None], 0.0), axis=1)
    lanes = -(-experts // 128) * 128
    weight_map = jnp.pad(weight_map, ((0, 0), (0, lanes - experts)))

    act = pl.pallas_call(
        functools.partial(gather_kernel, n_z, n_t, n_d),
        out_shape=jax.ShapeDtypeStruct((all_rows, mine * hidden_units), bf16),
        in_specs=[in_any, in_any, in_any, in_vmem, in_vmem, in_any, in_any],
        out_specs=in_vmem,
        scratch_shapes=[
            vmem((all_rows, full), bf16),
            vmem((all_rows, lanes), f32),
            vmem((2 * mine, width, hidden_units), bf16),
            vmem((2 * mine, all_rows, hidden_units), f32),
            dma((2 * mine,)),
            vmem((n_d * rows, depth), bf16),
            vmem((rows, width), bf16),
            vmem((depth, held), bf16),
            vmem((n_d * rows, held), bf16),
            vmem((n_t, rows, width), bf16),
            vmem((n_t, rows, 128), f32),
            dma, dma((2,)),
            dma((n_z,)), dma((n_z,)), dma((n_d,)), dma((n_d,)),
            dma((n_d,)), dma((n_d,)),
            dma((held // width, n_d)), dma((n_t,)),
            dma((n_t,)), dma((n_t,)),
            dma((n_z,)), dma((n_z,)),
            dma((n_t, n_z)), dma((n_t, n_z)),
            dma((n_d, n_t, n_z)), dma((n_d, n_t, n_z)),
        ],
        compiler_params=pltpu.CompilerParams(
            collective_id=0, has_side_effects=True, vmem_limit_bytes=60 * MIB
        ),
        name="project_gather_gate_up",
    )(attn, o_weight, residual, norm_gain.reshape(1, full), weight_map, w_gate, w_up)

    chunk = min(512, width)
    per_half = width // chunk
    steps = n_t * per_half
    group = n_z * rows
    return pl.pallas_call(
        functools.partial(reduce_kernel, n_z, n_t, n_d, chunk),
        out_shape=jax.ShapeDtypeStruct((rows, width), bf16),
        in_specs=[in_vmem, in_any],
        out_specs=in_vmem,
        scratch_shapes=[
            vmem((steps, mine * hidden_units, chunk), bf16),
            vmem((2, group, chunk), f32),
            vmem((steps, group, chunk), bf16),
            vmem((steps, group, chunk), bf16),
            vmem((n_t - 1, per_half, group, chunk), bf16),
            vmem((n_t - 1, per_half, group, chunk), bf16),
            vmem((per_half, group, chunk), f32),
            vmem((per_half, group, chunk), bf16),
            vmem((n_z, per_half, rows, chunk), bf16),
            dma((steps,)),
            dma((steps,)), dma((steps,)),
            dma((n_t, per_half)), dma((n_t, per_half)),
            dma((n_z, per_half)), dma((n_z, per_half)),
        ],
        compiler_params=pltpu.CompilerParams(
            collective_id=1, has_side_effects=True, vmem_limit_bytes=56 * MIB
        ),
        name="down_reduce",
    )(act, w_down.reshape(mine * hidden_units, full))


def solution(mesh):
    rows = ("groups", "expert", "dp")
    return jax.shard_map(
        on_device,
        mesh=mesh,
        in_specs=(
            P(rows, "tensor"),
            P("tensor", "dp"),
            P(rows, "tensor"),
            P(),
            P(rows, None),
            P(rows, None),
            P(("expert", "dp"), None, "tensor"),
            P(("expert", "dp"), None, "tensor"),
            P(("expert", "dp"), "tensor", None),
        ),
        out_specs=P(rows, "tensor"),
        check_vma=False,
    )
```
